32 devices in a mesh: groups: 2 (over y), sect: 16 (over z, x, core).
Axes of the slice: x: 2, y: 2, z: 4, core: 2. Of those that a mesh axis runs over, the one named last changes fastest.
Arguments:
- wavefunction: bfloat16 [512, 8, 128, 128], P(('groups', 'sect')), parts along dimension 0, may hold values from -6 to 6
- left_environment: bfloat16 [512, 2, 128, 128], P(('groups', 'sect')), parts along dimension 0, may hold values from -0.5 to 0.5
- right_environment: bfloat16 [128, 2, 128, 128], P(('groups', 'sect')), parts along dimension 0, may hold values from -0.5 to 0.5
- left_length: int32 [512], P(('groups', 'sect')), parts along dimension 0, may hold values from 64 to 128
- right_length: int32 [128], P(('groups', 'sect')), parts along dimension 0, may hold values from 64 to 128
- right_owner: int32 [512, 8], P(('groups', 'sect')), parts along dimension 0, may hold values from 0 to 15, all different within a row; in each aligned block of 16 rows (0 to 15, 16 to 31, ...) at most 8 rows name the same one
- right_slot: int32 [512, 8], P(('groups', 'sect')), parts along dimension 0, may hold values from 0 to 3
Outputs:
- hpsi: bfloat16 [512, 8, 128, 128], P(('groups', 'sect')), parts along dimension 0
The draws below stay inside these ranges and needn't reach their ends.
There are 2 independent parts, one for each index of `groups`. The reference program is written for one: setup_inputs(seed, part) draws one part's arguments, and reference() takes and returns one part's arrays. A program takes and returns all parts, laid end to end along the dimension named above; each array names one. Nothing has to cross between parts.
Inputs may be any that keep to these rules, and one draw needn't show every extreme that they name: `right_owner`: the 8 owners of one left sector are distinct; the 16 left sectors of one device name one owner at most 8 times in all, a bound that some block reaches by some device's left sectors.
All inputs are finite; a program needn't handle non-finite values.
Results may differ from the reference program's by a relative error of at most 0.0049.
Values may be sent and summed in bfloat16 or wider, within the bound.
No kernel may reach another device: no remote copies, remote signals or barrier semaphores. Data moves between devices by JAX's collectives and lax.ppermute only.
A program may use at most 128 MiB of HBM per device.

```python
import math
import jax
import jax.numpy as jnp
import numpy as np
from jax import lax

S = 128
K = 2
NNZ = 8
A_DEV = 16
B_DEV = 4
NA = 256
NB = 64
CAP = 8
N_SECT = 16


def plant(drawn, stream_key, low, top_value):
    shape = drawn.shape
    spot = [jax.random.randint(jax.random.fold_in(stream_key, axis), (), 0, shape[axis]) for axis in range(len(shape))]
    drawn = drawn.at[tuple(spot)].set(low)
    longest = shape.index(max(shape))
    spot[longest] = (spot[longest] + 1) % shape[longest]
    return drawn.at[tuple(spot)].set(top_value)


def shard_levels(stream_key, shape, split, smallest, largest):
    gain, own = 1.0, jax.random.fold_in(stream_key, 6)
    for axis_at, parts in split:
        draws = jnp.exp(jax.random.uniform(jax.random.fold_in(own, axis_at), (parts,), jnp.float32, smallest / len(split), largest / len(split)))
        gain = gain * jnp.repeat(draws, shape[axis_at] // parts).reshape([-1 if axis == axis_at else 1 for axis in range(len(shape))])
    return gain


def deal_out(own_key, own, number, rows, count, top, limit, slope):
    ranking = jax.random.permutation(own_key, count)
    crowded, usual = shares(count, rows * top, limit, slope, True), shares(count, rows * top, limit, slope, False)
    places = jnp.arange(count)

    def named(sizes, offset_by):
        used = int((sizes > 0).sum())
        fixed = max(1, used // 4)
        moved = fixed + (places - fixed + offset_by * (used - fixed)) % max(1, count - fixed)
        return jnp.zeros((count,), jnp.int32).at[ranking[jnp.where(places < fixed, places, moved)]].set(jnp.asarray(sizes, jnp.int32))

    sizes = jnp.where(number % 4 == 0, named(crowded, number // 4), named(usual, number - number // 4 - 1))
    mixed = jax.random.permutation(jax.random.fold_in(own, 3), count)
    giver, receiver = mixed[0:count // 2 * 2:2], mixed[1:count // 2 * 2:2]
    room = jnp.minimum(sizes[giver] - 1, limit - sizes[receiver]) // 2
    room = jnp.where((giver == ranking[0]) | (receiver == ranking[0]) | (sizes[receiver] == 0), 0, jnp.maximum(room, 0))
    moved = jax.random.randint(jax.random.fold_in(own, 4), (count // 2,), 0, 1 << 20) % (room + 1)
    sizes = sizes.at[giver].add(-moved).at[receiver].add(moved)
    labels = jnp.searchsorted(jnp.cumsum(sizes), jnp.arange(rows * top), side="right").astype(jnp.int32)
    listing = labels.reshape(top, rows).T
    listing = listing[jax.random.permutation(jax.random.fold_in(own, 1), rows)]
    offset_by = jax.random.randint(jax.random.fold_in(own, 2), (rows, 1), 0, top)
    return jnp.take_along_axis(listing, (jnp.arange(top)[None, :] + offset_by) % top, axis=1)


def shares(count, total, limit, lean, full):
    portions = [(1 << 20) // math.isqrt(rank ** lean) + 1 for rank in range(1, count + 1)]
    largest = limit if full else min(limit, max(-(-total // count), total * portions[0] // sum(portions)))
    least = 1 if total - largest >= count - 1 else 0
    counts, spare = [largest] + [least] * (count - 1), total - largest - least * (count - 1)
    while spare > 0:
        candidates = [i for i in range(1, count) if counts[i] < largest] or [i for i in range(1, count) if counts[i] < limit]
        mass, left = sum([portions[i] for i in candidates]), spare
        for i in candidates:
            addition = min(limit - counts[i], max(1, left * portions[i] // mass), spare)
            counts[i] = counts[i] + addition
            spare = spare - addition
    return np.array(counts)


def gaussian(own_key, dims, width, reach, cuts=(), kind=jnp.bfloat16):
    entries = width * jax.random.normal(own_key, dims, jnp.float32)
    if cuts:
        entries = entries * shard_levels(own_key, dims, cuts, -0.22, 0.18)
    return jnp.clip(entries, -reach, reach).astype(kind)


def setup_inputs(seed: int = 0, part: int = 0) -> dict:
    seeds = jax.random.split(jax.random.key(seed), 8)
    part_splits = jax.random.split(jax.random.fold_in(seeds[7], part), 8)
    wavefunction = gaussian(part_splits[0], (NA, NNZ, S, S), 1.0, 6.0, ((0, 16),))
    left_environment = gaussian(part_splits[1], (NA, K, S, S), S ** -0.5, 0.5, ((0, 16),))
    right_environment = gaussian(part_splits[2], (NB, K, S, S), S ** -0.5, 0.5, ((0, 16),))
    left_length = plant(jax.random.randint(part_splits[3], (NA,), S // 2, S + 1), jax.random.fold_in(part_splits[3], 1), S // 2, S).astype(jnp.int32)
    right_length = plant(jax.random.randint(part_splits[4], (NB,), S // 2, S + 1), jax.random.fold_in(part_splits[4], 1), S // 2, S).astype(jnp.int32)
    right_owner_keys = jax.random.split(jax.random.fold_in(part_splits[5], 1), NA // A_DEV)
    right_owner_turns = jax.random.permutation(jax.random.fold_in(part_splits[5], 3), NA // A_DEV)
    right_owner = jax.vmap(lambda own, number: deal_out(jax.random.fold_in(part_splits[5], 2), own, number, A_DEV, N_SECT, NNZ, CAP, 2))(right_owner_keys, right_owner_turns).reshape((NA, NNZ))
    right_slot = plant(jax.random.randint(part_splits[6], (NA, NNZ), 0, B_DEV), jax.random.fold_in(part_splits[6], 1), 0, B_DEV - 1).astype(jnp.int32)
    return {"wavefunction": wavefunction, "left_environment": left_environment, "right_environment": right_environment, "left_length": left_length, "right_length": right_length, "right_owner": right_owner, "right_slot": right_slot}


def mask_blocks(blocks, lengths):
    indices = jnp.arange(blocks.shape[-1], dtype=jnp.int32)
    live_rows = indices[None, :] < lengths[:, None]
    keep = live_rows[:, :, None] & live_rows[:, None, :]
    return jnp.where(keep[:, None, :, :], blocks, jnp.zeros_like(blocks))


def reference(wavefunction, left_environment, right_environment, left_length, right_length, right_owner, right_slot):
    right_live = mask_blocks(right_environment, right_length)
    right_sector = (right_owner * B_DEV + right_slot).astype(jnp.int32)
    groups_count = NA // A_DEV

    def one_group(pieces):
        waves, lefts, lengths, sectors = pieces
        left_live = mask_blocks(lefts, lengths)
        partial_value = jnp.einsum("akpq,ajqr->ajkpr", left_live.astype(jnp.float32), waves.astype(jnp.float32)).astype(jnp.bfloat16)
        chosen = jnp.take(right_live, sectors.reshape(-1).astype(jnp.int32), axis=0)
        chosen = chosen.reshape(sectors.shape[0], sectors.shape[1], K, S, S)
        result = jnp.einsum("ajkpr,ajkcr->ajpc", partial_value.astype(jnp.float32), chosen.astype(jnp.float32))
        return result.astype(jnp.bfloat16)

    pieces = (wavefunction.reshape(groups_count, A_DEV, NNZ, S, S),
              left_environment.reshape(groups_count, A_DEV, K, S, S),
              left_length.reshape(groups_count, A_DEV),
              right_sector.reshape(groups_count, A_DEV, NNZ))
    return lax.map(one_group, pieces).reshape(NA, NNZ, S, S)
```

```python
import functools

import jax
import jax.numpy as jnp
import numpy as np
from jax import lax
from jax.experimental import pallas as pl
from jax.experimental.pallas import tpu as pltpu
from jax.sharding import PartitionSpec as P

SMEM = pl.BlockSpec(memory_space=pltpu.SMEM)
VMEM = pl.BlockSpec(memory_space=pltpu.VMEM)
ANY = pl.BlockSpec(memory_space=pl.ANY)


def live(size, length):
    rows = lax.broadcasted_iota(jnp.int32, (size, size), 0)
    columns = lax.broadcasted_iota(jnp.int32, (size, size), 1)
    return (rows < length) & (columns < length)


def mask_kernel(length_ref, blocks_ref, out_ref):
    sectors, terms, size, _ = blocks_ref.shape
    for b in range(sectors):
        keep = live(size, length_ref[b])
        for k in range(terms):
            block = blocks_ref[b, k]
            out_ref[b, k] = jnp.where(keep, block, jnp.zeros_like(block))


def mask_right(lengths, blocks):
    return pl.pallas_call(
        mask_kernel,
        in_specs=[SMEM, VMEM],
        out_specs=VMEM,
        out_shape=pltpu.VMEM(blocks.shape, blocks.dtype),
        name="mask_right",
    )(lengths, blocks)


def partial_kernel(cap, slots, length_ref, place_ref, owner_ref, slot_ref, left_ref, wave_ref, partial_ref, work_ref, count_ref):
    step = pl.program_id(0)
    sectors, partners, size, _ = wave_ref.shape

    @pl.when(step == 0)
    def _():
        for c in range(count_ref.shape[0]):
            count_ref[c] = 0

    for s in range(sectors):
        a = step * sectors + s
        keep = live(size, length_ref[a])
        left = left_ref[s]
        left = jnp.where(keep[None], left, jnp.zeros_like(left))
        for j in range(partners):
            wave = wave_ref[s, j]
            for k in range(left.shape[0]):
                term = jnp.dot(left[k], wave, preferred_element_type=jnp.float32)
                partial_ref[a * partners + j, :, k * size:(k + 1) * size] = term.astype(partial_ref.dtype)
        for j in range(partners):
            chunk = place_ref[owner_ref[j, a]]
            filled = count_ref[chunk]
            count_ref[chunk] = filled + 1
            work_ref[chunk * cap + filled] = (a * partners + j) * slots + slot_ref[j, a]


def partials(cap, slots, lengths, place, owner, slot, left, wave):
    sectors, partners, size, _ = wave.shape
    terms, n = left.shape[1], place.shape[0]
    step = 2
    return pl.pallas_call(
        functools.partial(partial_kernel, cap, slots),
        grid=(sectors // step,),
        in_specs=[
            SMEM, SMEM, SMEM, SMEM,
            pl.BlockSpec((step, terms, size, size), lambda i: (i, 0, 0, 0)),
            pl.BlockSpec((step, partners, size, size), lambda i: (i, 0, 0, 0)),
        ],
        out_specs=[VMEM, SMEM, SMEM],
        out_shape=[
            pltpu.VMEM((sectors * partners, size, terms * size), wave.dtype),
            jax.ShapeDtypeStruct((n * cap,), jnp.int32),
            jax.ShapeDtypeStruct((n,), jnp.int32),
        ],
        compiler_params=pltpu.CompilerParams(vmem_limit_bytes=16 << 20),
        cost_estimate=pl.CostEstimate(
            flops=2 * sectors * partners * terms * size**3,
            bytes_accessed=2 * wave.size + 2 * left.size, transcendentals=0,
        ),
        name="partials",
    )(lengths, place, owner, slot, left, wave)


def product_kernel(first, cap, exact, slots, chunks, aliased, work_ref, count_ref, partial_ref, *refs):
    right_refs, out_ref, stage, sem = refs[:chunks], refs[chunks + aliased], refs[-2], refs[-1]
    partners = out_ref.shape[1]
    terms = right_refs[0].shape[1]

    def copy(at, index):
        return pltpu.make_async_copy(
            stage.at[at], out_ref.at[lax.div(index, partners), lax.rem(index, partners)], sem)

    for c in range(chunks):
        for i in range(cap):
            def item(c=c, i=i):
                entry = work_ref[(first + c) * cap + i]
                index, slot = lax.div(entry, slots), lax.rem(entry, slots)
                right = jnp.concatenate([right_refs[c][slot, k] for k in range(terms)], axis=1)
                stage[c * cap + i] = lax.dot_general(
                    partial_ref[index], right, (((1,), (1,)), ((), ())), preferred_element_type=jnp.float32,
                ).astype(stage.dtype)
                copy(c * cap + i, index).start()
            if exact:
                item()
            else:
                pl.when(i < count_ref[first + c])(item)
    if exact:
        whole = out_ref.at[pl.ds(0, chunks * cap // partners)]
        pltpu.make_async_copy(whole, whole, sem).wait()
    else:
        for c in range(chunks):
            for i in range(cap):
                @pl.when(i < count_ref[first + c])
                def _(c=c, i=i):
                    copy(c * cap + i, 0).wait()


def products(first, cap, exact, out_shape, work, count, partial_value, rights, out):
    chunks, aliased = len(rights), out is not None
    size = out_shape.shape[-1]
    rights = [pltpu.with_memory_space_constraint(r, pltpu.VMEM) for r in rights]
    partial_value = pltpu.with_memory_space_constraint(partial_value, pltpu.VMEM)
    return pl.pallas_call(
        functools.partial(product_kernel, first, cap, exact, rights[0].shape[0], chunks, aliased),
        in_specs=[SMEM, SMEM, VMEM] + [VMEM] * chunks + [ANY] * aliased,
        out_specs=ANY,
        out_shape=out_shape,
        scratch_shapes=[
            pltpu.VMEM((chunks * cap, size, size), out_shape.dtype),
            pltpu.SemaphoreType.DMA,
        ],
        input_output_aliases={3 + chunks: 0} if aliased else {},
        compiler_params=pltpu.CompilerParams(vmem_limit_bytes=16 << 20),
        cost_estimate=pl.CostEstimate(
            flops=2 * chunks * cap * 2 * size**3,
            bytes_accessed=2 * chunks * cap * size**2, transcendentals=0,
        ),
        name="products",
    )(work, count, partial_value, *rights, *([out] if aliased else []))


def local(n, wavefunction, left_environment, right_environment, left_length, right_length, right_owner, right_slot):
    sectors, partners = wavefunction.shape[:2]
    blocks = sectors * partners
    slots = right_environment.shape[0]
    cap = max(2, blocks // n)
    exact = cap * n == blocks
    chips = n // 2
    ring = list(range(0, chips, 2)) + list(range(chips - 1, 0, -2))
    at = {chip: i for i, chip in enumerate(ring)}
    onward = [(ring[i] * 2, ring[(i + 1) % chips] * 2) for i in range(chips)]
    onward += [(ring[i] * 2 + 1, ring[(i - 1) % chips] * 2 + 1) for i in range(chips)]
    across = [(d, d ^ 1) for d in range(n)]

    def origin(device, hop, other, via):
        chip, core = device // 2, device % 2
        carrier = core ^ via
        step = hop if carrier == 0 else -hop
        return ring[(at[chip] - step) % chips] * 2 + (carrier ^ other)

    plan = [(0, 0, 0), (0, 1, 0)]
    for hop in range(1, chips // 2 + 1):
        for other in (0, 1) if hop < chips // 2 else (0,):
            plan += [(hop, other, 0), (hop, other, 1)]
    place = np.zeros((n, n), np.int32)
    for device in range(n):
        for c, (hop, other, via) in enumerate(plan):
            place[device, origin(device, hop, other, via)] = c
    assert len(plan) == n

    me = lax.axis_index("sect")
    mine = mask_right(right_length, right_environment)
    send = functools.partial(lax.ppermute, axis_name="sect")
    chunks = [mine, send(mine, perm=across)]
    here = list(chunks)
    for hop in range(1, chips // 2 + 1):
        for other in (0, 1) if hop < chips // 2 else (0,):
            here[other] = send(here[other], perm=onward)
            chunks += [here[other], send(here[other], perm=across)]
    partial_value, work, count = partials(
        cap, slots, left_length, jnp.asarray(place)[me], right_owner.T, right_slot.T, left_environment, wavefunction)
    out_shape = jax.ShapeDtypeStruct(wavefunction.shape, wavefunction.dtype)
    out = None
    cuts = [0, 6, 10, 14, 16] if n == 16 else list(range(0, n, 16)) + [n]
    for low, high in zip(cuts, cuts[1:]):
        out = products(low, cap, exact, out_shape, work, count, partial_value, chunks[low:high], out)
    return out


def solution(mesh):
    split = ("groups", "sect")
    return jax.shard_map(
        functools.partial(local, mesh.shape["sect"]),
        mesh=mesh,
        in_specs=(
            P(split, None, None, None),
            P(split, None, None, None),
            P(split, None, None, None),
            P(split),
            P(split),
            P(split, None),
            P(split, None),
        ),
        out_specs=P(split, None, None, None),
        check_vma=False,
    )
```

```python
import functools

import jax
import jax.numpy as jnp
from jax import lax
from jax.experimental import pallas as pl
from jax.experimental.pallas import tpu as pltpu
from jax.sharding import PartitionSpec as P

SMEM = pl.BlockSpec(memory_space=pltpu.SMEM)
VMEM = pl.BlockSpec(memory_space=pltpu.VMEM)
ANY = pl.BlockSpec(memory_space=pl.ANY)
TOKEN = (8, 128)
GROUP = 2
PACE = 1150000000
LIMIT = pltpu.CompilerParams(vmem_limit_bytes=16 << 20)


def live(size, length):
    rows = lax.broadcasted_iota(jnp.int32, (size, size), 0)
    columns = lax.broadcasted_iota(jnp.int32, (size, size), 1)
    return (rows < length) & (columns < length)


def vmem(x):
    return pltpu.with_memory_space_constraint(x, pltpu.VMEM)


def hbm(x):
    return pltpu.with_memory_space_constraint(x, pltpu.HBM)


def mask_kernel(length_hbm, blocks_hbm, out_ref, length_ref, blocks_ref, sems):
    sectors, terms, size, _ = blocks_ref.shape
    lengths = pltpu.make_async_copy(length_hbm, length_ref, sems.at[sectors])
    blocks = [pltpu.make_async_copy(blocks_hbm.at[b], blocks_ref.at[b], sems.at[b]) for b in range(sectors)]
    lengths.start()
    for copy in blocks:
        copy.start()
    lengths.wait()
    for b in range(sectors):
        keep = live(size, length_ref[b])
        blocks[b].wait()
        for k in range(terms):
            block = blocks_ref[b, k]
            out_ref[b, k] = jnp.where(keep, block, jnp.zeros_like(block))


def mask_right(lengths, blocks):
    return pl.pallas_call(
        mask_kernel,
        in_specs=[ANY, ANY],
        out_specs=VMEM,
        out_shape=pltpu.VMEM(blocks.shape, blocks.dtype),
        scratch_shapes=[
            pltpu.SMEM(lengths.shape, jnp.int32),
            pltpu.VMEM(blocks.shape, blocks.dtype),
            pltpu.SemaphoreType.DMA((blocks.shape[0] + 1,)),
        ],
        compiler_params=pltpu.CompilerParams(vmem_limit_bytes=2 << 20),
        name="mask_right",
    )(hbm(lengths), hbm(blocks))


def join_kernel(block_ref, token_ref, out_ref):
    del block_ref, token_ref, out_ref


def join(block, token):
    return pl.pallas_call(
        join_kernel,
        in_specs=[VMEM, VMEM],
        out_specs=VMEM,
        out_shape=pltpu.VMEM(block.shape, block.dtype),
        input_output_aliases={0: 0},
        compiler_params=pltpu.CompilerParams(vmem_limit_bytes=1 << 20),
        name="join",
    )(vmem(block), vmem(token))


def multiply_left(low, high, length_ref, left_ref, wave_ref, partial_ref, ready=lambda a: None):
    terms, size = left_ref.shape[1:3]
    partners = wave_ref.shape[1]
    for a in range(low, high):
        ready(a)
        keep = live(size, length_ref[a])
        left = jnp.concatenate([jnp.where(keep, left_ref[a, k], 0) for k in range(terms)], axis=0)
        for j in range(0, partners, 2):
            wave = jnp.concatenate([wave_ref[a, j], wave_ref[a, j + 1]], axis=1)
            both = jnp.dot(left, wave, preferred_element_type=jnp.float32).astype(partial_ref.dtype)
            for i in range(2):
                for k in range(terms):
                    partial_ref[a * partners + j + i, :, k * size:(k + 1) * size] = (
                        both[k * size:(k + 1) * size, i * size:(i + 1) * size])


def opening_kernel(high, cap, slots, origins, length_hbm, owner_hbm, slot_hbm, left_hbm, wave_hbm,
                   partial_ref, token_ref, work_ref, count_ref, length_ref, left_ref, wave_ref,
                   owner_ref, slot_ref, place_ref, sems, scalar_sems):
    sectors, partners = wave_hbm.shape[:2]
    scalars = [
        pltpu.make_async_copy(source, target, scalar_sems.at[i])
        for i, (source, target) in enumerate(((length_hbm, length_ref), (owner_hbm, owner_ref), (slot_hbm, slot_ref)))]
    arrays = []
    for g in range(sectors // GROUP):
        at = pl.ds(g * GROUP, GROUP)
        arrays.append([
            pltpu.make_async_copy(left_hbm.at[at], left_ref.at[at], sems.at[0, g]),
            pltpu.make_async_copy(wave_hbm.at[at], wave_ref.at[at], sems.at[1, g])])
    for copy in scalars + sum(arrays, []):
        copy.start()
    token_ref[...] = jnp.zeros_like(token_ref)
    for c, origin in enumerate(origins(lax.axis_index("sect"))):
        place_ref[origin] = c
        count_ref[c] = 0
    for copy in scalars:
        copy.wait()
    for a in range(sectors):
        for j in range(partners):
            chunk = place_ref[owner_ref[j, a]]
            filled = count_ref[chunk]
            count_ref[chunk] = filled + 1
            work_ref[chunk * cap + filled] = (a * partners + j) * slots + slot_ref[j, a]

    def ready(a):
        if a % GROUP == 0:
            for copy in arrays[a // GROUP]:
                copy.wait()

    multiply_left(0, high, length_ref, left_ref, wave_ref, partial_ref, ready)
    for a in range(high, sectors):
        ready(a)


def opening(high, n, cap, slots, origins, lengths, owner, slot, left, wave):
    sectors, partners, size, _ = wave.shape
    terms = left.shape[1]
    return pl.pallas_call(
        functools.partial(opening_kernel, high, cap, slots, origins),
        in_specs=[ANY] * 5,
        out_specs=[VMEM, VMEM, SMEM, SMEM, SMEM, VMEM, VMEM],
        out_shape=[
            pltpu.VMEM((sectors * partners, size, terms * size), wave.dtype),
            pltpu.VMEM(TOKEN, jnp.float32),
            pltpu.SMEM((n * cap,), jnp.int32),
            pltpu.SMEM((n,), jnp.int32),
            pltpu.SMEM(lengths.shape, jnp.int32),
            pltpu.VMEM(left.shape, left.dtype),
            pltpu.VMEM(wave.shape, wave.dtype),
        ],
        scratch_shapes=[
            pltpu.SMEM(owner.shape, jnp.int32),
            pltpu.SMEM(slot.shape, jnp.int32),
            pltpu.SMEM((n,), jnp.int32),
            pltpu.SemaphoreType.DMA((2, sectors // GROUP)),
            pltpu.SemaphoreType.DMA((3,)),
        ],
        compiler_params=LIMIT,
        cost_estimate=pl.CostEstimate(flops=PACE, bytes_accessed=0, transcendentals=0),
        name="opening",
    )(*map(hbm, (lengths, owner, slot, left, wave)))


def partial_kernel(low, high, length_ref, left_ref, wave_ref, _, partial_ref, token_ref):
    token_ref[...] = jnp.zeros_like(token_ref)
    multiply_left(low, high, length_ref, left_ref, wave_ref, partial_ref)


def partials(low, high, lengths, left, wave, before):
    return pl.pallas_call(
        functools.partial(partial_kernel, low, high),
        in_specs=[SMEM, VMEM, VMEM, VMEM],
        out_specs=[VMEM, VMEM],
        out_shape=[pltpu.VMEM(before.shape, before.dtype), pltpu.VMEM(TOKEN, jnp.float32)],
        input_output_aliases={3: 0},
        compiler_params=LIMIT,
        cost_estimate=pl.CostEstimate(flops=PACE, bytes_accessed=0, transcendentals=0),
        name="partials",
    )(lengths, vmem(left), vmem(wave), vmem(before))


def product_kernel(first, cap, exact, chunks, flush, given, marked, work_ref, count_ref, partial_ref, *refs):
    right_refs, refs = refs[:chunks], refs[chunks:]
    refs = refs[given:]
    stage, refs = refs[0], refs[1:]
    slots, terms = right_refs[0].shape[:2]
    if marked:
        refs[0][...] = jnp.zeros_like(refs[0])
        refs = refs[1:]

    def each(low, high, body):
        for c in range(low, high):
            for i in range(cap):
                if exact:
                    body(c, i)
                else:
                    pl.when(i < count_ref[c])(functools.partial(body, c, i))

    def where(c, i):
        entry = work_ref[c * cap + i]
        return lax.div(entry, slots), lax.rem(entry, slots)

    def item(c, i):
        index, slot = where(c, i)
        right = jnp.concatenate([right_refs[c - first][slot, k] for k in range(terms)], axis=1)
        stage[index] = lax.dot_general(
            partial_ref[index], right, (((1,), (1,)), ((), ())), preferred_element_type=jnp.float32,
        ).astype(stage.dtype)

    if flush is None:
        each(first, first + chunks, item)
        return
    out_ref, sem = refs

    def copy(c, i):
        index, _ = where(c, i)
        return pltpu.make_async_copy(stage.at[index], out_ref.at[index], sem)

    def start(c, i):
        copy(c, i).start()

    def both(c, i):
        item(c, i)
        start(c, i)

    each(flush, first, start)
    each(first, first + chunks, both)
    if exact:
        whole = out_ref.at[pl.ds(0, (first + chunks - flush) * cap)]
        pltpu.make_async_copy(whole, whole, sem).wait()
    else:
        each(flush, first + chunks, lambda c, i: copy(c, i).wait())


def products(first, cap, exact, flush, marked, work, count, partial_value, rights, stage, out):
    blocks, size, _ = partial_value.shape
    chunks = len(rights)
    operands = [vmem(stage)] if stage is not None else []
    specs = [VMEM] * len(operands)
    aliases = {3 + chunks: 0} if operands else {}
    out_specs, out_shape, scratch = [VMEM], [pltpu.VMEM((blocks, size, size), partial_value.dtype)], []
    if marked:
        out_specs.append(VMEM)
        out_shape.append(pltpu.VMEM(TOKEN, jnp.float32))
    if flush is not None:
        out_specs.append(ANY)
        out_shape.append(jax.ShapeDtypeStruct((blocks, size, size), partial_value.dtype))
        scratch.append(pltpu.SemaphoreType.DMA)
        if out is not None:
            aliases[3 + chunks + len(operands)] = 1 + marked
            operands.append(out)
            specs.append(ANY)
    result = pl.pallas_call(
        functools.partial(product_kernel, first, cap, exact, chunks, flush, len(operands), marked),
        in_specs=[SMEM, SMEM, VMEM] + [VMEM] * chunks + specs,
        out_specs=out_specs,
        out_shape=out_shape,
        scratch_shapes=scratch,
        input_output_aliases=aliases,
        compiler_params=LIMIT,
        cost_estimate=pl.CostEstimate(flops=PACE, bytes_accessed=0, transcendentals=0),
        name="products",
    )(work, count, vmem(partial_value), *map(vmem, rights), *operands)
    stage, *result = result
    token = result.pop(0) if marked else None
    return stage, token, result[0] if result else out


def local(n, wavefunction, left_environment, right_environment, left_length, right_length, right_owner, right_slot):
    sectors, partners = wavefunction.shape[:2]
    blocks = sectors * partners
    cap = max(2, blocks // n)
    exact = cap * n == blocks
    chips = n // 2
    hops = chips // 2

    def chip_at(i):
        i = i % chips
        return 2 * i if i < hops else 2 * (chips - 1 - i) + 1

    onward = [(chip_at(i) * 2, chip_at(i + 1) * 2) for i in range(chips)]
    onward += [(chip_at(i) * 2 + 1, chip_at(i - 1) * 2 + 1) for i in range(chips)]
    across = [(d, d ^ 1) for d in range(n)]

    plan = [(0, 0, 0), (0, 1, 0)]
    for hop in range(1, hops + 1):
        plan += [(hop, 0, 0), (hop, 0, 1)]
        if hop < hops:
            plan += [(hop, 1, 0), (hop, 1, 1)]

    def origins(device):
        core, chip = lax.rem(device, 2), lax.div(device, 2)
        half = lax.div(chip, 2)
        at = jnp.where(lax.rem(chip, 2) == 0, half, chips - 1 - half)
        for hop, other, via in plan:
            carrier = core if via == 0 else 1 - core
            i = lax.rem(at + jnp.where(carrier == 0, chips - hop, hop), chips)
            source = jnp.where(i < hops, 2 * i, 2 * (chips - 1 - i) + 1)
            yield 2 * source + (carrier if other == 0 else 1 - carrier)

    def send(block, perm):
        return lax.ppermute(block, "sect", perm)

    first = mask_right(right_length, right_environment)
    held = {(0, 0, 0): first, (1, 0, 0): send(first, onward)}
    held[0, 1, 0] = send(first, across)
    held[1, 1, 0] = send(held[0, 1, 0], onward)
    part = work = count = stage = out = None
    cuts = [sectors // 2, 3 * sectors // 4, sectors]
    done = 0
    windows = [(hop, other) for hop in range(1, hops + 1) for other in (0, 1) if hop < hops or not other]
    for at, (hop, other) in enumerate(windows):
        if not at:
            part, token, work, count, lengths, left, wave = opening(
                cuts[0], n, cap, right_environment.shape[0], origins, left_length, right_owner.T, right_slot.T, left_environment, wavefunction)
        elif at < len(cuts):
            part, token = partials(cuts[at - 1], cuts[at], lengths, left, wave, part)
        else:
            upto = 2 * at if at + 1 < len(windows) else 2 * at + 1
            stage, token, out = products(
                done, cap, exact, 0 if at + 1 == len(windows) else None, True, work, count, part,
                [held[p] for p in plan[done:upto]], stage, out)
            done = upto
        here = held[hop, other, 0] = join(held[hop, other, 0], token)
        if hop + 1 + other <= hops:
            held[hop + 1, other, 0] = send(here, onward)
        held[hop, other, 1] = send(here, across)
    flushed = done
    for upto in (n - 1, n):
        stage, token, out = products(
            done, cap, exact, flushed, False, work, count, part, [held[p] for p in plan[done:upto]], stage, out)
        done = flushed = upto
    return out.reshape(wavefunction.shape)


def solution(mesh):
    split = ("groups", "sect")
    return jax.shard_map(
        functools.partial(local, mesh.shape["sect"]),
        mesh=mesh,
        in_specs=(
            P(split, None, None, None),
            P(split, None, None, None),
            P(split, None, None, None),
            P(split),
            P(split),
            P(split, None),
            P(split, None),
        ),
        out_specs=P(split, None, None, None),
        check_vma=False,
    )
```

```python
import functools

import jax
import jax.numpy as jnp
from jax import lax
from jax.experimental import pallas as pl
from jax.experimental.pallas import tpu as pltpu
from jax.sharding import PartitionSpec as P

SMEM = pl.BlockSpec(memory_space=pltpu.SMEM)
VMEM = pl.BlockSpec(memory_space=pltpu.VMEM)
ANY = pl.BlockSpec(memory_space=pl.ANY)
TOKEN = (8, 128)
PACE = 1150000000
LIMIT = pltpu.CompilerParams(vmem_limit_bytes=16 << 20)


def live(size, length):
    rows = lax.broadcasted_iota(jnp.int32, (size, size), 0)
    columns = lax.broadcasted_iota(jnp.int32, (size, size), 1)
    return (rows < length) & (columns < length)


def vmem(x):
    return pltpu.with_memory_space_constraint(x, pltpu.VMEM)


def hbm(x):
    return pltpu.with_memory_space_constraint(x, pltpu.HBM)


def mask_kernel(length_hbm, blocks_hbm, left_hbm, owner_hbm, slot_hbm, out_ref, left_ref, owner_ref, slot_ref, length_ref, blocks_ref, sems):
    sectors, terms, size, _ = blocks_ref.shape
    pairs = [(length_hbm, length_ref), (left_hbm, left_ref), (owner_hbm, owner_ref), (slot_hbm, slot_ref)]
    scalars = [pltpu.make_async_copy(source, target, sems.at[sectors + i]) for i, (source, target) in enumerate(pairs)]
    blocks = [pltpu.make_async_copy(blocks_hbm.at[b], blocks_ref.at[b], sems.at[b]) for b in range(sectors)]
    for copy in scalars[:1] + blocks + scalars[1:]:
        copy.start()
    scalars[0].wait()
    for b in range(sectors):
        keep = live(size, length_ref[b])
        blocks[b].wait()
        for k in range(terms):
            block = blocks_ref[b, k]
            out_ref[b, k] = jnp.where(keep, block, jnp.zeros_like(block))
    for copy in scalars[1:]:
        copy.wait()


def mask_right(lengths, blocks, *scalars):
    return pl.pallas_call(
        mask_kernel,
        in_specs=[ANY] * 5,
        out_specs=[VMEM, SMEM, SMEM, SMEM],
        out_shape=[pltpu.VMEM(blocks.shape, blocks.dtype)] + [pltpu.SMEM(x.shape, x.dtype) for x in scalars],
        scratch_shapes=[
            pltpu.SMEM(lengths.shape, jnp.int32),
            pltpu.VMEM(blocks.shape, blocks.dtype),
            pltpu.SemaphoreType.DMA((blocks.shape[0] + 1 + len(scalars),)),
        ],
        compiler_params=pltpu.CompilerParams(vmem_limit_bytes=2 << 20),
        cost_estimate=pl.CostEstimate(flops=10 * PACE, bytes_accessed=0, transcendentals=0),
        name="mask_right",
    )(*map(hbm, (lengths, blocks, *scalars)))


def join_kernel(block_ref, token_ref, out_ref):
    del block_ref, token_ref, out_ref


def join(block, token):
    return pl.pallas_call(
        join_kernel,
        in_specs=[VMEM, VMEM],
        out_specs=VMEM,
        out_shape=pltpu.VMEM(block.shape, block.dtype),
        input_output_aliases={0: 0},
        compiler_params=pltpu.CompilerParams(vmem_limit_bytes=1 << 20),
        name="join",
    )(vmem(block), vmem(token))


def multiply_left(low, high, length_ref, left_ref, wave_ref, partial_ref, ready=lambda a: None):
    terms, size = left_ref.shape[1:3]
    partners = wave_ref.shape[1]
    for a in range(low, high):
        ready(a)
        keep = live(size, length_ref[a])
        left = jnp.concatenate([jnp.where(keep, left_ref[a, k], 0) for k in range(terms)], axis=0)
        for j in range(0, partners, 2):
            wave = jnp.concatenate([wave_ref[a, j], wave_ref[a, j + 1]], axis=1)
            both = jnp.dot(left, wave, preferred_element_type=jnp.float32).astype(partial_ref.dtype)
            for i in range(2):
                for k in range(terms):
                    partial_ref[a * partners + j + i, :, k * size:(k + 1) * size] = (
                        both[k * size:(k + 1) * size, i * size:(i + 1) * size])


def opening_kernel(high, cap, slots, origins, length_ref, owner_ref, slot_ref, left_ref, wave_ref,
                   partial_ref, token_ref, work_ref, count_ref, place_ref):
    sectors, partners = wave_ref.shape[:2]
    token_ref[...] = jnp.zeros_like(token_ref)
    for c, origin in enumerate(origins(lax.axis_index("sect"))):
        place_ref[origin] = c
        count_ref[c] = 0
    for a in range(sectors):
        for j in range(partners):
            chunk = place_ref[owner_ref[j, a]]
            filled = count_ref[chunk]
            count_ref[chunk] = filled + 1
            work_ref[chunk * cap + filled] = (a * partners + j) * slots + slot_ref[j, a]
    multiply_left(0, high, length_ref, left_ref, wave_ref, partial_ref)


def opening(high, n, cap, slots, origins, lengths, owner, slot, left, wave):
    sectors, partners, size, _ = wave.shape
    terms = left.shape[1]
    return pl.pallas_call(
        functools.partial(opening_kernel, high, cap, slots, origins),
        in_specs=[SMEM] * 3 + [VMEM] * 2,
        out_specs=[VMEM, VMEM, SMEM, SMEM],
        out_shape=[
            pltpu.VMEM((sectors * partners, size, terms * size), wave.dtype),
            pltpu.VMEM(TOKEN, jnp.float32),
            pltpu.SMEM((n * cap,), jnp.int32),
            pltpu.SMEM((n,), jnp.int32),
        ],
        scratch_shapes=[pltpu.SMEM((n,), jnp.int32)],
        compiler_params=LIMIT,
        cost_estimate=pl.CostEstimate(flops=PACE, bytes_accessed=0, transcendentals=0),
        name="opening",
    )(lengths, owner, slot, left, wave)


def partial_kernel(low, high, length_ref, left_ref, wave_ref, _, partial_ref, token_ref):
    token_ref[...] = jnp.zeros_like(token_ref)
    multiply_left(low, high, length_ref, left_ref, wave_ref, partial_ref)


def partials(low, high, lengths, left, wave, before):
    return pl.pallas_call(
        functools.partial(partial_kernel, low, high),
        in_specs=[SMEM, VMEM, VMEM, VMEM],
        out_specs=[VMEM, VMEM],
        out_shape=[pltpu.VMEM(before.shape, before.dtype), pltpu.VMEM(TOKEN, jnp.float32)],
        input_output_aliases={3: 0},
        compiler_params=LIMIT,
        cost_estimate=pl.CostEstimate(flops=PACE, bytes_accessed=0, transcendentals=0),
        name="partials",
    )(lengths, left, wave, vmem(before))


def product_kernel(first, cap, exact, chunks, flush, given, marked, work_ref, count_ref, partial_ref, *refs):
    right_refs, refs = refs[:chunks], refs[chunks:]
    refs = refs[given:]
    stage, refs = refs[0], refs[1:]
    slots, terms = right_refs[0].shape[:2]
    if marked:
        refs[0][...] = jnp.zeros_like(refs[0])
        refs = refs[1:]

    def each(low, high, body):
        for c in range(low, high):
            for i in range(cap):
                if exact:
                    body(c, i)
                else:
                    pl.when(i < count_ref[c])(functools.partial(body, c, i))

    def where(c, i):
        entry = work_ref[c * cap + i]
        return lax.div(entry, slots), lax.rem(entry, slots)

    def item(c, i):
        index, slot = where(c, i)
        right = jnp.concatenate([right_refs[c - first][slot, k] for k in range(terms)], axis=1)
        stage[index] = lax.dot_general(
            partial_ref[index], right, (((1,), (1,)), ((), ())), preferred_element_type=jnp.float32,
        ).astype(stage.dtype)

    if flush is None:
        each(first, first + chunks, item)
        return
    out_ref, sem = refs

    def copy(c, i):
        index, _ = where(c, i)
        return pltpu.make_async_copy(stage.at[index], out_ref.at[index], sem)

    def start(c, i):
        copy(c, i).start()

    def both(c, i):
        item(c, i)
        start(c, i)

    each(flush, first, start)
    each(first, first + chunks, both)
    if exact:
        whole = out_ref.at[pl.ds(0, (first + chunks - flush) * cap)]
        pltpu.make_async_copy(whole, whole, sem).wait()
    else:
        each(flush, first + chunks, lambda c, i: copy(c, i).wait())


def products(first, cap, exact, flush, marked, work, count, partial_value, rights, stage, out):
    blocks, size, _ = partial_value.shape
    chunks = len(rights)
    operands = [vmem(stage)] if stage is not None else []
    specs = [VMEM] * len(operands)
    aliases = {3 + chunks: 0} if operands else {}
    out_specs, out_shape, scratch = [VMEM], [pltpu.VMEM((blocks, size, size), partial_value.dtype)], []
    if marked:
        out_specs.append(VMEM)
        out_shape.append(pltpu.VMEM(TOKEN, jnp.float32))
    if flush is not None:
        out_specs.append(ANY)
        out_shape.append(jax.ShapeDtypeStruct((blocks, size, size), partial_value.dtype))
        scratch.append(pltpu.SemaphoreType.DMA)
        if out is not None:
            aliases[3 + chunks + len(operands)] = 1 + marked
            operands.append(out)
            specs.append(ANY)
    result = pl.pallas_call(
        functools.partial(product_kernel, first, cap, exact, chunks, flush, len(operands), marked),
        in_specs=[SMEM, SMEM, VMEM] + [VMEM] * chunks + specs,
        out_specs=out_specs,
        out_shape=out_shape,
        scratch_shapes=scratch,
        input_output_aliases=aliases,
        compiler_params=LIMIT,
        cost_estimate=pl.CostEstimate(flops=PACE, bytes_accessed=0, transcendentals=0),
        name="products",
    )(work, count, vmem(partial_value), *map(vmem, rights), *operands)
    stage, *result = result
    token = result.pop(0) if marked else None
    return stage, token, result[0] if result else out


def local(n, wavefunction, left_environment, right_environment, left_length, right_length, right_owner, right_slot):
    sectors, partners = wavefunction.shape[:2]
    blocks = sectors * partners
    cap = max(2, blocks // n)
    exact = cap * n == blocks
    chips = n // 2
    hops = chips // 2

    def chip_at(i):
        i = i % chips
        return 2 * i if i < hops else 2 * (chips - 1 - i) + 1

    onward = [(chip_at(i) * 2, chip_at(i + 1) * 2) for i in range(chips)]
    onward += [(chip_at(i) * 2 + 1, chip_at(i - 1) * 2 + 1) for i in range(chips)]
    across = [(d, d ^ 1) for d in range(n)]

    plan = [(0, 0, 0), (0, 1, 0)]
    for hop in range(1, hops + 1):
        plan += [(hop, 0, 0), (hop, 0, 1)]
        if hop < hops:
            plan += [(hop, 1, 0), (hop, 1, 1)]

    def origins(device):
        core, chip = lax.rem(device, 2), lax.div(device, 2)
        half = lax.div(chip, 2)
        at = jnp.where(lax.rem(chip, 2) == 0, half, chips - 1 - half)
        for hop, other, via in plan:
            carrier = core if via == 0 else 1 - core
            i = lax.rem(at + jnp.where(carrier == 0, chips - hop, hop), chips)
            source = jnp.where(i < hops, 2 * i, 2 * (chips - 1 - i) + 1)
            yield 2 * source + (carrier if other == 0 else 1 - carrier)

    def send(block, perm):
        return lax.ppermute(block, "sect", perm)

    first, lengths, owner, slot = mask_right(
        right_length, right_environment, left_length, right_owner.T, right_slot.T)
    held = {(0, 0, 0): first, (1, 0, 0): send(first, onward)}
    held[0, 1, 0] = send(first, across)
    held[1, 1, 0] = send(held[0, 1, 0], onward)
    part = work = count = stage = out = None
    cuts = [sectors // 2, 3 * sectors // 4, sectors]
    done = 0
    windows = [(hop, other) for hop in range(1, hops + 1) for other in (0, 1) if hop < hops or not other]
    for at, (hop, other) in enumerate(windows):
        if not at:
            part, token, work, count = opening(
                cuts[0], n, cap, right_environment.shape[0], origins, lengths, owner, slot, left_environment, wavefunction)
        elif at < len(cuts):
            part, token = partials(cuts[at - 1], cuts[at], lengths, left_environment, wavefunction, part)
        else:
            upto = 2 * at if at + 1 < len(windows) else 2 * at + 1
            stage, token, out = products(
                done, cap, exact, 0 if at + 1 == len(windows) else None, True, work, count, part,
                [held[p] for p in plan[done:upto]], stage, out)
            done = upto
        here = held[hop, other, 0] = join(held[hop, other, 0], token)
        if hop + 1 + other <= hops:
            held[hop + 1, other, 0] = send(here, onward)
        held[hop, other, 1] = send(here, across)
    flushed = done
    for upto in (n - 1, n):
        stage, token, out = products(
            done, cap, exact, flushed, False, work, count, part, [held[p] for p in plan[done:upto]], stage, out)
        done = flushed = upto
    return out.reshape(wavefunction.shape)


def solution(mesh):
    split = ("groups", "sect")
    return jax.shard_map(
        functools.partial(local, mesh.shape["sect"]),
        mesh=mesh,
        in_specs=(
            P(split, None, None, None),
            P(split, None, None, None),
            P(split, None, None, None),
            P(split),
            P(split),
            P(split, None),
            P(split, None),
        ),
        out_specs=P(split, None, None, None),
        check_vma=False,
    )
```

```python
import functools

import jax
import jax.numpy as jnp
from jax import lax
from jax.experimental import pallas as pl
from jax.experimental.pallas import tpu as pltpu
from jax.sharding import PartitionSpec as P

SMEM = pl.BlockSpec(memory_space=pltpu.SMEM)
VMEM = pl.BlockSpec(memory_space=pltpu.VMEM)
ANY = pl.BlockSpec(memory_space=pl.ANY)
TOKEN = (8, 128)
PACE = 1150000000
PACK = PACE
SMALL = pltpu.CompilerParams(vmem_limit_bytes=2 << 20)
LIMIT = pltpu.CompilerParams(vmem_limit_bytes=16 << 20)


def live(size, length):
    rows = lax.broadcasted_iota(jnp.int32, (size, size), 0)
    columns = lax.broadcasted_iota(jnp.int32, (size, size), 1)
    return (rows < length) & (columns < length)


def vmem(x):
    return pltpu.with_memory_space_constraint(x, pltpu.VMEM)


def hbm(x):
    return pltpu.with_memory_space_constraint(x, pltpu.HBM)


def mask_kernel(length_hbm, blocks_hbm, left_hbm, owner_hbm, slot_hbm, out_ref, left_ref, owner_ref, slot_ref, length_ref, blocks_ref, sems):
    sectors, terms, size, _ = blocks_ref.shape
    pairs = [(length_hbm, length_ref), (left_hbm, left_ref), (owner_hbm, owner_ref), (slot_hbm, slot_ref)]
    scalars = [pltpu.make_async_copy(source, target, sems.at[sectors + i]) for i, (source, target) in enumerate(pairs)]
    blocks = [pltpu.make_async_copy(blocks_hbm.at[b], blocks_ref.at[b], sems.at[b]) for b in range(sectors)]
    for copy in scalars[:1] + blocks + scalars[1:]:
        copy.start()
    scalars[0].wait()
    for b in range(sectors):
        keep = live(size, length_ref[b])
        blocks[b].wait()
        for k in range(terms):
            block = blocks_ref[b, k]
            out_ref[b, k] = jnp.where(keep, block, jnp.zeros_like(block))
    for copy in scalars[1:]:
        copy.wait()


def mask_right(lengths, blocks, *scalars):
    return pl.pallas_call(
        mask_kernel,
        in_specs=[ANY] * 5,
        out_specs=[VMEM, SMEM, SMEM, SMEM],
        out_shape=[pltpu.VMEM(blocks.shape, blocks.dtype)] + [pltpu.SMEM(x.shape, x.dtype) for x in scalars],
        scratch_shapes=[
            pltpu.SMEM(lengths.shape, jnp.int32),
            pltpu.VMEM(blocks.shape, blocks.dtype),
            pltpu.SemaphoreType.DMA((blocks.shape[0] + 1 + len(scalars),)),
        ],
        compiler_params=SMALL,
        cost_estimate=pl.CostEstimate(flops=11500000000, bytes_accessed=0, transcendentals=0),
        name="mask_right",
    )(*map(hbm, (lengths, blocks, *scalars)))


def join_kernel(block_ref, *refs):
    del block_ref, refs


def join(block, *tokens, cost=0):
    return pl.pallas_call(
        join_kernel,
        in_specs=[VMEM] * (1 + len(tokens)),
        out_specs=VMEM,
        out_shape=pltpu.VMEM(block.shape, block.dtype),
        input_output_aliases={0: 0},
        compiler_params=SMALL,
        cost_estimate=pl.CostEstimate(flops=cost, bytes_accessed=0, transcendentals=0),
        name="join",
    )(vmem(block), *map(vmem, tokens))


def pack_kernel(*refs):
    *block_refs, out_ref, token_ref = refs
    token_ref[...] = jnp.zeros_like(token_ref)
    for i, block_ref in enumerate(block_refs):
        out_ref[i] = block_ref[...]


def pack(*blocks):
    return pl.pallas_call(
        pack_kernel,
        in_specs=[VMEM] * len(blocks),
        out_specs=[VMEM, VMEM],
        out_shape=[
            pltpu.VMEM((len(blocks), *blocks[0].shape), blocks[0].dtype),
            pltpu.VMEM(TOKEN, jnp.float32)],
        compiler_params=SMALL,
        cost_estimate=pl.CostEstimate(flops=PACK, bytes_accessed=0, transcendentals=0),
        name="pack",
    )(*map(vmem, blocks))


def multiply_left(low, high, length_ref, left_ref, wave_ref, partial_ref, ready=lambda a: None):
    terms, size = left_ref.shape[1:3]
    partners = wave_ref.shape[1]
    for a in range(low, high):
        ready(a)
        keep = live(size, length_ref[a])
        left = jnp.concatenate([jnp.where(keep, left_ref[a, k], 0) for k in range(terms)], axis=0)
        for j in range(0, partners, 2):
            wave = jnp.concatenate([wave_ref[a, j], wave_ref[a, j + 1]], axis=1)
            both = jnp.dot(left, wave, preferred_element_type=jnp.float32).astype(partial_ref.dtype)
            for i in range(2):
                for k in range(terms):
                    partial_ref[a * partners + j + i, :, k * size:(k + 1) * size] = (
                        both[k * size:(k + 1) * size, i * size:(i + 1) * size])


def opening_kernel(high, cap, slots, origins, length_ref, owner_ref, slot_ref, left_ref, wave_ref,
                   partial_ref, token_ref, work_ref, count_ref, place_ref):
    sectors, partners = wave_ref.shape[:2]
    token_ref[...] = jnp.zeros_like(token_ref)
    for c, origin in enumerate(origins(lax.axis_index("sect"))):
        place_ref[origin] = c
        count_ref[c] = 0
    for a in range(sectors):
        for j in range(partners):
            chunk = place_ref[owner_ref[j, a]]
            filled = count_ref[chunk]
            count_ref[chunk] = filled + 1
            work_ref[chunk * cap + filled] = (a * partners + j) * slots + slot_ref[j, a]
    multiply_left(0, high, length_ref, left_ref, wave_ref, partial_ref)


def opening(high, n, cap, slots, origins, lengths, owner, slot, left, wave):
    sectors, partners, size, _ = wave.shape
    terms = left.shape[1]
    return pl.pallas_call(
        functools.partial(opening_kernel, high, cap, slots, origins),
        in_specs=[SMEM] * 3 + [VMEM] * 2,
        out_specs=[VMEM, VMEM, SMEM, SMEM],
        out_shape=[
            pltpu.VMEM((sectors * partners, size, terms * size), wave.dtype),
            pltpu.VMEM(TOKEN, jnp.float32),
            pltpu.SMEM((n * cap,), jnp.int32),
            pltpu.SMEM((n,), jnp.int32),
        ],
        scratch_shapes=[pltpu.SMEM((n,), jnp.int32)],
        compiler_params=LIMIT,
        cost_estimate=pl.CostEstimate(flops=PACE, bytes_accessed=0, transcendentals=0),
        name="opening",
    )(lengths, owner, slot, left, wave)


def partial_kernel(low, high, length_ref, left_ref, wave_ref, _, partial_ref, token_ref):
    token_ref[...] = jnp.zeros_like(token_ref)
    multiply_left(low, high, length_ref, left_ref, wave_ref, partial_ref)


def partials(low, high, lengths, left, wave, before):
    return pl.pallas_call(
        functools.partial(partial_kernel, low, high),
        in_specs=[SMEM, VMEM, VMEM, VMEM],
        out_specs=[VMEM, VMEM],
        out_shape=[pltpu.VMEM(before.shape, before.dtype), pltpu.VMEM(TOKEN, jnp.float32)],
        input_output_aliases={3: 0},
        compiler_params=LIMIT,
        cost_estimate=pl.CostEstimate(flops=PACE, bytes_accessed=0, transcendentals=0),
        name="partials",
    )(lengths, left, wave, vmem(before))


def product_kernel(first, cap, exact, places, flush, given, marked, work_ref, count_ref, partial_ref, *refs):
    chunks = len(places)
    right_refs = [ref if at is None else ref.at[at] for ref, at in zip(refs, places)]
    refs = refs[chunks:]
    refs = refs[given:]
    stage, refs = refs[0], refs[1:]
    slots, terms = right_refs[0].shape[:2]
    if marked:
        refs[0][...] = jnp.zeros_like(refs[0])
        refs = refs[1:]

    def each(low, high, body):
        for c in range(low, high):
            for i in range(cap):
                if exact:
                    body(c, i)
                else:
                    pl.when(i < count_ref[c])(functools.partial(body, c, i))

    def where(c, i):
        entry = work_ref[c * cap + i]
        return lax.div(entry, slots), lax.rem(entry, slots)

    def item(c, i):
        index, slot = where(c, i)
        right = jnp.concatenate([right_refs[c - first][slot, k] for k in range(terms)], axis=1)
        stage[index] = lax.dot_general(
            partial_ref[index], right, (((1,), (1,)), ((), ())), preferred_element_type=jnp.float32,
        ).astype(stage.dtype)

    if flush is None:
        each(first, first + chunks, item)
        return
    out_ref, sem = refs

    def copy(c, i):
        index, _ = where(c, i)
        return pltpu.make_async_copy(stage.at[index], out_ref.at[index], sem)

    def start(c, i):
        copy(c, i).start()

    def both(c, i):
        item(c, i)
        start(c, i)

    each(flush, first, start)
    each(first, first + chunks, both)
    if exact:
        whole = out_ref.at[pl.ds(0, (first + chunks - flush) * cap)]
        pltpu.make_async_copy(whole, whole, sem).wait()
    else:
        each(flush, first + chunks, lambda c, i: copy(c, i).wait())


def products(first, cap, exact, flush, marked, work, count, partial_value, rights, stage, out):
    blocks, size, _ = partial_value.shape
    rights, places = zip(*rights)
    chunks = len(rights)
    operands = [vmem(stage)] if stage is not None else []
    specs = [VMEM] * len(operands)
    aliases = {3 + chunks: 0} if operands else {}
    out_specs, out_shape, scratch = [VMEM], [pltpu.VMEM((blocks, size, size), partial_value.dtype)], []
    if marked:
        out_specs.append(VMEM)
        out_shape.append(pltpu.VMEM(TOKEN, jnp.float32))
    if flush is not None:
        out_specs.append(ANY)
        out_shape.append(jax.ShapeDtypeStruct((blocks, size, size), partial_value.dtype))
        scratch.append(pltpu.SemaphoreType.DMA)
        if out is not None:
            aliases[3 + chunks + len(operands)] = 1 + marked
            operands.append(out)
            specs.append(ANY)
    result = pl.pallas_call(
        functools.partial(product_kernel, first, cap, exact, places, flush, len(operands), marked),
        in_specs=[SMEM, SMEM, VMEM] + [VMEM] * chunks + specs,
        out_specs=out_specs,
        out_shape=out_shape,
        scratch_shapes=scratch,
        input_output_aliases=aliases,
        compiler_params=LIMIT,
        cost_estimate=pl.CostEstimate(flops=PACE, bytes_accessed=0, transcendentals=0),
        name="products",
    )(work, count, vmem(partial_value), *map(vmem, rights), *operands)
    stage, *result = result
    token = result.pop(0) if marked else None
    return stage, token, result[0] if result else out


def local(n, wavefunction, left_environment, right_environment, left_length, right_length, right_owner, right_slot):
    sectors, partners = wavefunction.shape[:2]
    blocks = sectors * partners
    cap = max(2, blocks // n)
    exact = cap * n == blocks
    chips = n // 2
    hops = chips // 2

    def chip_at(i):
        i = i % chips
        return 2 * i if i < hops else 2 * (chips - 1 - i) + 1

    onward = [(chip_at(i) * 2, chip_at(i + 1) * 2) for i in range(chips)]
    onward += [(chip_at(i) * 2 + 1, chip_at(i - 1) * 2 + 1) for i in range(chips)]
    across = [(d, d ^ 1) for d in range(n)]

    plan = [(0, 0, 0), (0, 1, 0)]
    for hop in range(1, hops):
        plan += [(hop, 0, 0), (hop, 1, 0), (hop, 0, 1), (hop, 1, 1)]
    plan += [(hops, 0, 0), (hops, 0, 1)]

    def origins(device):
        core, chip = lax.rem(device, 2), lax.div(device, 2)
        half = lax.div(chip, 2)
        at = jnp.where(lax.rem(chip, 2) == 0, half, chips - 1 - half)
        for hop, other, via in plan:
            carrier = core if via == 0 else 1 - core
            i = lax.rem(at + jnp.where(carrier == 0, chips - hop, hop), chips)
            source = jnp.where(i < hops, 2 * i, 2 * (chips - 1 - i) + 1)
            yield 2 * source + (carrier if other == 0 else 1 - carrier)

    def send(block, perm):
        return lax.ppermute(block, "sect", perm)

    first, lengths, owner, slot = mask_right(
        right_length, right_environment, left_length, right_owner.T, right_slot.T)
    first = join(first, cost=11500000000)
    held = {(0, 0, 0): first, (1, 0, 0): send(first, onward)}
    held[0, 1, 0] = send(first, across)
    held[1, 1, 0] = send(held[0, 1, 0], onward)
    within = {}
    part = work = count = stage = out = None
    cuts = [sectors // 2, 3 * sectors // 4, sectors]
    done, packs = 0, []

    def chunks(low, high):
        return [(held[p], within.get(p)) for p in plan[low:high]]

    windows = [(hop, other) for hop in range(1, hops + 1) for other in (0, 1) if hop < hops or not other]
    for at, (hop, other) in enumerate(windows):
        if not at:
            part, token, work, count = opening(
                cuts[0], n, cap, right_environment.shape[0], origins, lengths, owner, slot, left_environment, wavefunction)
        elif at < len(cuts):
            part, token = partials(cuts[at - 1], cuts[at], lengths, left_environment, wavefunction, part)
        else:
            upto = 2 * at - 2 * (at + 1 < len(windows))
            stage, token, out = products(
                done, cap, exact, 0 if at + 1 == len(windows) else None, True, work, count, part,
                chunks(done, upto), stage, out)
            done = upto
        here = held[hop, other, 0] = join(held[hop, other, 0], token, *packs, cost=PACE)
        packs = []
        if hop + 1 + other <= hops:
            held[hop + 1, other, 0] = send(here, onward)
        if other:
            both, mark = pack(held[hop, 0, 0], here)
            packs = [mark]
            held[hop, 0, 1] = held[hop, 1, 1] = send(both, across)
            within[hop, 0, 1], within[hop, 1, 1] = 0, 1
    held[hops, 0, 1] = send(held[hops, 0, 0], across)
    flushed = done
    for upto in (n - 1, n):
        stage, token, out = products(
            done, cap, exact, flushed, False, work, count, part, chunks(done, upto), stage, out)
        done = flushed = upto
    return out.reshape(wavefunction.shape)


def solution(mesh):
    split = ("groups", "sect")
    return jax.shard_map(
        functools.partial(local, mesh.shape["sect"]),
        mesh=mesh,
        in_specs=(
            P(split, None, None, None),
            P(split, None, None, None),
            P(split, None, None, None),
            P(split),
            P(split),
            P(split, None),
            P(split, None),
        ),
        out_specs=P(split, None, None, None),
        check_vma=False,
    )
```

```python
import functools

import jax
import jax.numpy as jnp
from jax import lax
from jax.experimental import pallas as pl
from jax.experimental.pallas import tpu as pltpu
from jax.sharding import PartitionSpec as P

SMEM = pl.BlockSpec(memory_space=pltpu.SMEM)
VMEM = pl.BlockSpec(memory_space=pltpu.VMEM)
ANY = pl.BlockSpec(memory_space=pl.ANY)
TOKEN = (8, 128)
PACE = 1150000000
PACK = PACE
SMALL = pltpu.CompilerParams(vmem_limit_bytes=2 << 20)
LIMIT = pltpu.CompilerParams(vmem_limit_bytes=16 << 20)


def live(size, length):
    rows = lax.broadcasted_iota(jnp.int32, (size, size), 0)
    columns = lax.broadcasted_iota(jnp.int32, (size, size), 1)
    return (rows < length) & (columns < length)


def vmem(x):
    return pltpu.with_memory_space_constraint(x, pltpu.VMEM)


def hbm(x):
    return pltpu.with_memory_space_constraint(x, pltpu.HBM)


def mask_kernel(length_hbm, blocks_hbm, left_hbm, owner_hbm, slot_hbm, out_ref, left_ref, owner_ref, slot_ref, length_ref, blocks_ref, sems):
    sectors, terms, size, _ = blocks_ref.shape
    pairs = [(length_hbm, length_ref), (left_hbm, left_ref), (owner_hbm, owner_ref), (slot_hbm, slot_ref)]
    scalars = [pltpu.make_async_copy(source, target, sems.at[sectors + i]) for i, (source, target) in enumerate(pairs)]
    blocks = [pltpu.make_async_copy(blocks_hbm.at[b], blocks_ref.at[b], sems.at[b]) for b in range(sectors)]
    for copy in scalars[:1] + blocks + scalars[1:]:
        copy.start()
    scalars[0].wait()
    for b in range(sectors):
        keep = live(size, length_ref[b])
        blocks[b].wait()
        for k in range(terms):
            block = blocks_ref[b, k]
            out_ref[b, k] = jnp.where(keep, block, jnp.zeros_like(block))
    for copy in scalars[1:]:
        copy.wait()


def mask_right(lengths, blocks, *scalars):
    return pl.pallas_call(
        mask_kernel,
        in_specs=[ANY] * 5,
        out_specs=[VMEM, SMEM, SMEM, SMEM],
        out_shape=[pltpu.VMEM(blocks.shape, blocks.dtype)] + [pltpu.SMEM(x.shape, x.dtype) for x in scalars],
        scratch_shapes=[
            pltpu.SMEM(lengths.shape, jnp.int32),
            pltpu.VMEM(blocks.shape, blocks.dtype),
            pltpu.SemaphoreType.DMA((blocks.shape[0] + 1 + len(scalars),)),
        ],
        compiler_params=SMALL,
        cost_estimate=pl.CostEstimate(flops=1150000000, bytes_accessed=0, transcendentals=0),
        name="mask_right",
    )(*map(hbm, (lengths, blocks, *scalars)))


def join_kernel(block_ref, *refs):
    del block_ref, refs


def join(block, *tokens, cost=0):
    return pl.pallas_call(
        join_kernel,
        in_specs=[VMEM] * (1 + len(tokens)),
        out_specs=VMEM,
        out_shape=pltpu.VMEM(block.shape, block.dtype),
        input_output_aliases={0: 0},
        compiler_params=SMALL,
        cost_estimate=pl.CostEstimate(flops=cost, bytes_accessed=0, transcendentals=0),
        name="join",
    )(vmem(block), *map(vmem, tokens))


def remask_kernel(block_ref, length_ref, *refs):
    out_ref = refs[-1]
    sectors, terms, size, _ = block_ref.shape
    for b in range(sectors):
        keep = live(size, jnp.broadcast_to(length_ref[:, b:b + 1], (size, size)))
        for k in range(terms):
            block = block_ref[b, k]
            out_ref[b, k] = jnp.where(keep, block, jnp.zeros_like(block))


def remask(block, lengths, *tokens, cost=0):
    return pl.pallas_call(
        remask_kernel,
        in_specs=[VMEM] * (2 + len(tokens)),
        out_specs=VMEM,
        out_shape=pltpu.VMEM(block.shape, block.dtype),
        input_output_aliases={0: 0},
        compiler_params=SMALL,
        cost_estimate=pl.CostEstimate(flops=cost, bytes_accessed=0, transcendentals=0),
        name="remask",
    )(vmem(block), vmem(lengths), *map(vmem, tokens))


def pack_kernel(*refs):
    *block_refs, out_ref, token_ref = refs
    token_ref[...] = jnp.zeros_like(token_ref)
    for i, block_ref in enumerate(block_refs):
        out_ref[i] = block_ref[...]


def pack(*blocks):
    return pl.pallas_call(
        pack_kernel,
        in_specs=[VMEM] * len(blocks),
        out_specs=[VMEM, VMEM],
        out_shape=[
            pltpu.VMEM((len(blocks), *blocks[0].shape), blocks[0].dtype),
            pltpu.VMEM(TOKEN, jnp.float32)],
        compiler_params=SMALL,
        cost_estimate=pl.CostEstimate(flops=PACK, bytes_accessed=0, transcendentals=0),
        name="pack",
    )(*map(vmem, blocks))


def multiply_left(low, high, length_ref, left_ref, wave_ref, partial_ref, ready=lambda a: None):
    terms, size = left_ref.shape[1:3]
    partners = wave_ref.shape[1]
    for a in range(low, high):
        ready(a)
        keep = live(size, length_ref[a])
        left = jnp.concatenate([jnp.where(keep, left_ref[a, k], 0) for k in range(terms)], axis=0)
        for j in range(0, partners, 2):
            wave = jnp.concatenate([wave_ref[a, j], wave_ref[a, j + 1]], axis=1)
            both = jnp.dot(left, wave, preferred_element_type=jnp.float32).astype(partial_ref.dtype)
            for i in range(2):
                for k in range(terms):
                    partial_ref[a * partners + j + i, :, k * size:(k + 1) * size] = (
                        both[k * size:(k + 1) * size, i * size:(i + 1) * size])


def opening_kernel(high, cap, slots, origins, length_ref, owner_ref, slot_ref, left_ref, wave_ref, _,
                   partial_ref, token_ref, work_ref, count_ref, place_ref):
    sectors, partners = wave_ref.shape[:2]
    token_ref[...] = jnp.zeros_like(token_ref)
    for c, origin in enumerate(origins(lax.axis_index("sect"))):
        place_ref[origin] = c
        count_ref[c] = 0
    for a in range(sectors):
        for j in range(partners):
            chunk = place_ref[owner_ref[j, a]]
            filled = count_ref[chunk]
            count_ref[chunk] = filled + 1
            work_ref[chunk * cap + filled] = (a * partners + j) * slots + slot_ref[j, a]
    multiply_left(0, high, length_ref, left_ref, wave_ref, partial_ref)


def opening(high, n, cap, slots, origins, lengths, owner, slot, left, wave, after):
    sectors, partners, size, _ = wave.shape
    terms = left.shape[1]
    return pl.pallas_call(
        functools.partial(opening_kernel, high, cap, slots, origins),
        in_specs=[SMEM] * 3 + [VMEM] * 3,
        out_specs=[VMEM, VMEM, SMEM, SMEM],
        out_shape=[
            pltpu.VMEM((sectors * partners, size, terms * size), wave.dtype),
            pltpu.VMEM(TOKEN, jnp.float32),
            pltpu.SMEM((n * cap,), jnp.int32),
            pltpu.SMEM((n,), jnp.int32),
        ],
        scratch_shapes=[pltpu.SMEM((n,), jnp.int32)],
        compiler_params=LIMIT,
        cost_estimate=pl.CostEstimate(flops=PACE, bytes_accessed=0, transcendentals=0),
        name="opening",
    )(lengths, owner, slot, left, wave, vmem(after))


def partial_kernel(low, high, length_ref, left_ref, wave_ref, _, partial_ref, token_ref):
    token_ref[...] = jnp.zeros_like(token_ref)
    multiply_left(low, high, length_ref, left_ref, wave_ref, partial_ref)


def partials(low, high, lengths, left, wave, before):
    return pl.pallas_call(
        functools.partial(partial_kernel, low, high),
        in_specs=[SMEM, VMEM, VMEM, VMEM],
        out_specs=[VMEM, VMEM],
        out_shape=[pltpu.VMEM(before.shape, before.dtype), pltpu.VMEM(TOKEN, jnp.float32)],
        input_output_aliases={3: 0},
        compiler_params=LIMIT,
        cost_estimate=pl.CostEstimate(flops=PACE, bytes_accessed=0, transcendentals=0),
        name="partials",
    )(lengths, left, wave, vmem(before))


def product_kernel(first, cap, exact, places, flush, given, marked, work_ref, count_ref, partial_ref, *refs):
    chunks = len(places)
    right_refs = [ref if at is None else ref.at[at] for ref, at in zip(refs, places)]
    refs = refs[chunks:]
    refs = refs[given:]
    stage, refs = refs[0], refs[1:]
    slots, terms = right_refs[0].shape[:2]
    if marked:
        refs[0][...] = jnp.zeros_like(refs[0])
        refs = refs[1:]

    def each(low, high, body):
        for c in range(low, high):
            for i in range(cap):
                if exact:
                    body(c, i)
                else:
                    pl.when(i < count_ref[c])(functools.partial(body, c, i))

    def where(c, i):
        entry = work_ref[c * cap + i]
        return lax.div(entry, slots), lax.rem(entry, slots)

    def item(c, i):
        index, slot = where(c, i)
        right = jnp.concatenate([right_refs[c - first][slot, k] for k in range(terms)], axis=1)
        stage[index] = lax.dot_general(
            partial_ref[index], right, (((1,), (1,)), ((), ())), preferred_element_type=jnp.float32,
        ).astype(stage.dtype)

    if flush is None:
        each(first, first + chunks, item)
        return
    out_ref, sem = refs

    def copy(c, i):
        index, _ = where(c, i)
        return pltpu.make_async_copy(stage.at[index], out_ref.at[index], sem)

    def start(c, i):
        copy(c, i).start()

    def both(c, i):
        item(c, i)
        start(c, i)

    each(flush, first, start)
    each(first, first + chunks, both)
    if exact:
        whole = out_ref.at[pl.ds(0, (first + chunks - flush) * cap)]
        pltpu.make_async_copy(whole, whole, sem).wait()
    else:
        each(flush, first + chunks, lambda c, i: copy(c, i).wait())


def products(first, cap, exact, flush, marked, work, count, partial_value, rights, stage, out):
    blocks, size, _ = partial_value.shape
    rights, places = zip(*rights)
    chunks = len(rights)
    operands = [vmem(stage)] if stage is not None else []
    specs = [VMEM] * len(operands)
    aliases = {3 + chunks: 0} if operands else {}
    out_specs, out_shape, scratch = [VMEM], [pltpu.VMEM((blocks, size, size), partial_value.dtype)], []
    if marked:
        out_specs.append(VMEM)
        out_shape.append(pltpu.VMEM(TOKEN, jnp.float32))
    if flush is not None:
        out_specs.append(ANY)
        out_shape.append(jax.ShapeDtypeStruct((blocks, size, size), partial_value.dtype))
        scratch.append(pltpu.SemaphoreType.DMA)
        if out is not None:
            aliases[3 + chunks + len(operands)] = 1 + marked
            operands.append(out)
            specs.append(ANY)
    result = pl.pallas_call(
        functools.partial(product_kernel, first, cap, exact, places, flush, len(operands), marked),
        in_specs=[SMEM, SMEM, VMEM] + [VMEM] * chunks + specs,
        out_specs=out_specs,
        out_shape=out_shape,
        scratch_shapes=scratch,
        input_output_aliases=aliases,
        compiler_params=LIMIT,
        cost_estimate=pl.CostEstimate(flops=PACE, bytes_accessed=0, transcendentals=0),
        name="products",
    )(work, count, vmem(partial_value), *map(vmem, rights), *operands)
    stage, *result = result
    token = result.pop(0) if marked else None
    return stage, token, result[0] if result else out


def local(n, wavefunction, left_environment, right_environment, left_length, right_length, right_owner, right_slot):
    sectors, partners = wavefunction.shape[:2]
    blocks = sectors * partners
    cap = max(2, blocks // n)
    exact = cap * n == blocks
    chips = n // 2
    hops = chips // 2

    def chip_at(i):
        i = i % chips
        return 2 * i if i < hops else 2 * (chips - 1 - i) + 1

    onward = [(chip_at(i) * 2, chip_at(i + 1) * 2) for i in range(chips)]
    onward += [(chip_at(i) * 2 + 1, chip_at(i - 1) * 2 + 1) for i in range(chips)]
    across = [(d, d ^ 1) for d in range(n)]

    plan = [(0, 0, 0), (0, 1, 0)]
    for hop in range(1, hops):
        plan += [(hop, 0, 0), (hop, 1, 0), (hop, 0, 1), (hop, 1, 1)]
    plan += [(hops, 0, 0), (hops, 0, 1)]

    def origins(device):
        core, chip = lax.rem(device, 2), lax.div(device, 2)
        half = lax.div(chip, 2)
        at = jnp.where(lax.rem(chip, 2) == 0, half, chips - 1 - half)
        for hop, other, via in plan:
            carrier = core if via == 0 else 1 - core
            i = lax.rem(at + jnp.where(carrier == 0, chips - hop, hop), chips)
            source = jnp.where(i < hops, 2 * i, 2 * (chips - 1 - i) + 1)
            yield 2 * source + (carrier if other == 0 else 1 - carrier)

    def send(block, perm):
        return lax.ppermute(block, "sect", perm)

    first, lengths, owner, slot = mask_right(
        right_length, right_environment, left_length, right_owner.T, right_slot.T)
    row = right_length[None]
    beside, beside_row = send(right_environment, across), send(row, across)
    came = send(row, onward)
    held = {(0, 0, 0): first, (1, 0, 0): send(right_environment, onward)}
    held[0, 1, 0] = remask(beside, beside_row, cost=0)
    held[1, 1, 0] = send(held[0, 1, 0], onward)
    within = {}
    part = work = count = stage = out = None
    cuts = [sectors // 2, sectors]
    done, packs = 0, []

    def chunks(low, high):
        return [(held[p], within.get(p)) for p in plan[low:high]]

    windows = [(hop, other) for hop in range(1, hops + 1) for other in (0, 1) if hop < hops or not other]
    for at, (hop, other) in enumerate(windows):
        if not at:
            token = first
        elif at == 1:
            part, token, work, count = opening(
                cuts[0], n, cap, right_environment.shape[0], origins, lengths, owner, slot, left_environment, wavefunction,
                held[1, 0, 0])
        elif at == 2:
            part, token = partials(cuts[0], cuts[1], lengths, left_environment, wavefunction, part)
        else:
            upto = 2 * at - 2 * (at + 1 < len(windows))
            stage, token, out = products(
                done, cap, exact, 0 if at + 1 == len(windows) else None, True, work, count, part,
                chunks(done, upto), stage, out)
            done = upto
        if at:
            here = join(held[hop, other, 0], token, *packs, cost=PACE)
        else:
            here = remask(held[hop, other, 0], came, token, cost=PACE)
        held[hop, other, 0] = here
        packs = []
        if hop + 1 + other <= hops:
            held[hop + 1, other, 0] = send(here, onward)
        if other:
            both, mark = pack(held[hop, 0, 0], here)
            packs = [mark]
            held[hop, 0, 1] = held[hop, 1, 1] = send(both, across)
            within[hop, 0, 1], within[hop, 1, 1] = 0, 1
    held[hops, 0, 1] = send(held[hops, 0, 0], across)
    flushed = done
    for upto in (n - 1, n):
        stage, token, out = products(
            done, cap, exact, flushed, False, work, count, part, chunks(done, upto), stage, out)
        done = flushed = upto
    return out.reshape(wavefunction.shape)


def solution(mesh):
    split = ("groups", "sect")
    return jax.shard_map(
        functools.partial(local, mesh.shape["sect"]),
        mesh=mesh,
        in_specs=(
            P(split, None, None, None),
            P(split, None, None, None),
            P(split, None, None, None),
            P(split),
            P(split),
            P(split, None),
            P(split, None),
        ),
        out_specs=P(split, None, None, None),
        check_vma=False,
    )
```
